512 devices in a mesh: frame: 64 (over y, z_hi, core), row: 8 (over x, z_lo).
Axes of the slice: x: 4, y: 8, z: 8 (z_hi: 4, z_lo: 2; z = z_hi * 2 + z_lo), core: 2. Of those that a mesh axis runs over, the one named last changes fastest.
Arguments:
- latents: bfloat16 [64, 1024, 640], P('frame', 'row'), may hold values from -6 to 6
- norm_gain: float32 [640], replicated, may hold values from 0.1 to 1.9
- w_query: bfloat16 [640, 640], replicated
- w_key: bfloat16 [640, 640], replicated, as said below
- w_value: bfloat16 [640, 640], replicated, may hold values from -0.25 to 0.25
- w_out: bfloat16 [640, 640], replicated, may hold values from -2 to 2
Outputs:
- mixed: bfloat16 [64, 1024, 640], P('frame', 'row')
The draws below stay inside these ranges and needn't reach their ends.
Inputs may be any that keep to these rules, and one draw needn't show every extreme that they name: `w_key`: a weight matrix scaled for 640 inputs.
All inputs are finite; a program needn't handle non-finite values.
Results may differ from the reference program's by a relative error of at most 0.015.
Values may be sent and summed in bfloat16 or wider, within the bound.
No kernel may reach another device: no remote copies, remote signals or barrier semaphores. Data moves between devices by JAX's collectives and lax.ppermute only.
A program may use at most 128 MiB of HBM per device.

```python
import jax
import jax.numpy as jnp
from jax import lax

C = 640
HEADS = 8
P_SIZE = 1024
FRAMES = 64


def shared_key(key):
    return jax.random.normal(key, (C, C), jnp.float32) * C ** (-0.5)


def draw_w_key(key, part):
    base = shared_key(key)
    return base.astype(jnp.bfloat16)


def draw_w_query(key, part):
    key = jax.random.fold_in(key, 23)
    noise = jax.random.normal(key, (C, C), jnp.float32) * C ** (-0.5)
    return noise.astype(jnp.bfloat16)


def level_of(own_key, extent, pieces, smallest, largest):
    def one(dim, parts):
        draws = jax.random.uniform(jax.random.fold_in(jax.random.fold_in(own_key, 6), dim), (parts,), jnp.float32, smallest / len(pieces), largest / len(pieces))
        return jnp.repeat(jnp.exp(draws), extent[dim] // parts).reshape((-1,) + (1,) * (len(extent) - dim - 1))

    level = one(*pieces[0])
    for cut in pieces[1:]:
        level = level * one(*cut)
    return level


def scatter_about(own_key, dims, scale, bound, pieces=(), kind=jnp.bfloat16):
    array = jax.random.normal(own_key, dims, jnp.float32) * scale
    if len(pieces) > 0:
        array = level_of(own_key, dims, pieces, -0.22, 0.18) * array
    return jnp.clip(array, min=-bound, max=bound).astype(kind)


def setup_inputs(seed: int = 0) -> dict:
    splits = jax.random.split(jax.random.key(seed), 7)
    return {
        "latents": scatter_about(splits[0], (FRAMES, P_SIZE, C), 1.0, 6.0, ((0, 64), (1, 8))),
        "norm_gain": jnp.clip(1.0 + 0.18 * jax.random.normal(splits[1], (C,), jnp.float32), 0.1, 1.9),
        "w_query": draw_w_query(jax.random.fold_in(splits[6], 71), 0),
        "w_key": draw_w_key(jax.random.fold_in(splits[6], 71), 0),
        "w_value": scatter_about(splits[4], (C, C), C ** -0.5, 0.25),
        "w_out": scatter_about(splits[5], (C, C), (C // 64) ** -0.5, 2.0),
    }


def layer_norm(latents, norm_gain):
    values = latents.astype(jnp.float32)
    center = values - lax.optimization_barrier(jnp.mean(values, axis=-1, keepdims=True))
    spread = lax.optimization_barrier(jnp.mean(center * center, axis=-1, keepdims=True))
    return (center * lax.rsqrt(spread + 1e-05) * norm_gain).astype(jnp.bfloat16)

def project(normed, weight):
    flat = normed.reshape(-1, normed.shape[-1])
    return jnp.dot(flat, weight, preferred_element_type=jnp.float32).astype(jnp.bfloat16).reshape(normed.shape[:-1] + (weight.shape[1],))

def reference(latents, norm_gain, w_query, w_key, w_value, w_out):
    normed = layer_norm(latents, norm_gain)
    query = project(normed, w_query)
    key = project(normed, w_key)
    value = project(normed, w_value)
    head_dim = C // HEADS

    def one_frame(index):
        index = index.astype(jnp.int32)
        before = jnp.maximum(index - 1, 0).astype(jnp.int32)
        keys = jnp.concatenate([key[index], key[before], key[0]], axis=0)
        values = jnp.concatenate([value[index], value[before], value[0]], axis=0)
        qh = query[index].astype(jnp.float32).reshape(P_SIZE, HEADS, head_dim)
        kh = keys.astype(jnp.float32).reshape(3 * P_SIZE, HEADS, head_dim)
        vh = values.astype(jnp.float32).reshape(3 * P_SIZE, HEADS, head_dim)
        scores = jnp.einsum('qhd,khd->hqk', qh, kh) / jnp.sqrt(jnp.float32(head_dim))
        weights = jax.nn.softmax(scores, axis=-1).astype(jnp.bfloat16)
        attended = jnp.einsum('hqk,khd->qhd', weights.astype(jnp.float32), vh)
        return attended.reshape(P_SIZE, C).astype(jnp.bfloat16)
    attended = lax.map(one_frame, jnp.arange(FRAMES, dtype=jnp.int32))
    update = jnp.dot(attended.reshape(-1, C), w_out, preferred_element_type=jnp.float32).reshape(FRAMES, P_SIZE, C)
    return (latents.astype(jnp.float32) + update).astype(jnp.bfloat16)
```

```python
import math

import jax
import jax.numpy as jnp
from jax import lax
from jax.experimental import pallas as pl
from jax.experimental.pallas import tpu as pltpu
from jax.sharding import PartitionSpec as P

HEADS = 8
SPREAD = 16
VMEM = 32 * 2**20

ROUNDS = (
    ((4, 0, 0), (2, 0, 0), (6, 0, 0)),
    ((0, 2, 0), (0, 1, 0), (0, 3, 0)),
    ((1, 0, 0), (1, 0, 1), (0, 0, 1)),
)
SIZES = (8, 4, 2)


def index_of(place):
    return (place[0] * SIZES[1] + place[1]) * SIZES[2] + place[2]


def spread_plan():
    held = [(0, 0, 0)]
    plan = []
    for steps in ROUNDS:
        perms = []
        fresh = []
        for step in steps:
            pairs = []
            for place in held:
                to = tuple((a + b) % n for a, b, n in zip(place, step, SIZES))
                pairs.append((index_of(place), index_of(to)))
                fresh.append(to)
            perms.append(pairs)
        held = held + fresh
        plan.append(perms)
    return plan


def normed_of(values, gain):
    values = values.astype(jnp.float32)
    center = values - jnp.mean(values, axis=-1, keepdims=True)
    spread = jnp.mean(center * center, axis=-1, keepdims=True)
    return (center * lax.rsqrt(spread + 1e-05) * gain).astype(jnp.bfloat16)


def project(normed, weight):
    return jnp.dot(normed, weight, preferred_element_type=jnp.float32)


def by_head(rows):
    channels, positions = rows.shape[1], rows.shape[0]
    return rows.astype(jnp.bfloat16).T.reshape(HEADS, channels // HEADS, positions)


def own_kernel(flag, own, prior, gain, w_query, w_key, w_value, out):
    positions, channels = own.shape
    head = channels // HEADS
    scale = math.log2(math.e) / math.sqrt(head)
    before = jnp.where(flag[0] == 0, own[...].astype(jnp.float32), prior[...].astype(jnp.float32))
    normed = normed_of(own[...], gain[...])
    both = jnp.concatenate([normed, normed_of(before, gain[...])], axis=0)
    out[:, :head, :] = by_head(project(normed, w_query[...]) * scale)
    key = project(both, w_key[...])
    value = project(both, w_value[...])
    out[:, head : 2 * head, :] = by_head(key[:positions])
    out[:, 2 * head : 3 * head, :] = by_head(value[:positions])
    out[:, 3 * head : 4 * head, :] = by_head(key[positions:])
    out[:, 4 * head :, :] = by_head(value[positions:])


def pick_kernel(flag, held, one, two, three, out):
    for which, ref in enumerate((held, one, two, three)):

        @pl.when(flag[0] == which)
        def _():
            out[...] = ref[...]


def first_kernel(flag, held, one, two, three, gain, w_key, w_value, out, latents):
    pick_kernel(flag, held, one, two, three, latents)
    head = latents.shape[1] // HEADS
    normed = normed_of(latents[...], gain[...])
    out[:, :head, :] = by_head(project(normed, w_key[...]))
    out[:, head:, :] = by_head(project(normed, w_value[...]))


def joined(ref, start, size, blocks):
    return jnp.concatenate([ref[b, start : start + size, :] for b in blocks], axis=1)


def ones_row(count):
    return (lax.broadcasted_iota(jnp.int32, (SPREAD, count), 0) == 0).astype(jnp.float32).astype(jnp.bfloat16)


def scores_of(key, query):
    return lax.dot_general(key, query, (((0,), (0,)), ((), ())), preferred_element_type=jnp.float32)


GROUP = 4


def near_kernel(rows, peak, total):
    blocks, _, width = rows.shape
    head = rows.shape[1] // 5
    every = range(blocks)
    keys = [joined(rows, start * head, head, every) for start in (1, 3)]
    values = [
        jnp.concatenate([joined(rows, start * head, head, every), ones_row(blocks * width)], axis=0)
        for start in (2, 4)
    ]
    for g in range(0, blocks, GROUP):
        query = joined(rows, 0, head, range(g, g + GROUP))
        scores = [scores_of(key, query) for key in keys]
        top = jnp.maximum(*[jnp.max(s, axis=0, keepdims=True) for s in scores])
        span = slice(g * width, (g + GROUP) * width)
        peak[:, span] = jnp.broadcast_to(top, (8, GROUP * width))
        total[:, span] = sum(
            jnp.dot(value, jnp.exp2(s - top).astype(jnp.bfloat16), preferred_element_type=jnp.float32)
            for value, s in zip(values, scores)
        )


def far_kernel(rows, first, peak, total, out):
    blocks, _, width = rows.shape
    head = rows.shape[1] // 5
    every = range(blocks)
    key = joined(first, 0, head, every)
    value = jnp.concatenate([joined(first, head, head, every), ones_row(blocks * width)], axis=0)
    for g in range(0, blocks, GROUP):
        query = joined(rows, 0, head, range(g, g + GROUP))
        scores = scores_of(key, query)
        span = slice(g * width, (g + GROUP) * width)
        before = peak[:1, span]
        top = jnp.maximum(jnp.max(scores, axis=0, keepdims=True), before)
        weights = jnp.exp2(scores - top).astype(jnp.bfloat16)
        both = total[:, span] * jnp.exp2(before - top) + jnp.dot(
            value, weights, preferred_element_type=jnp.float32
        )
        attended = (both[:head] / both[head : head + 1]).astype(jnp.bfloat16)
        for b in range(GROUP):
            out[g + b] = attended[:, b * width : (b + 1) * width]


def mix_kernel(attended, latents, w_out, out):
    heads, head, positions = attended.shape
    rows = attended[...].reshape(heads * head, positions).T
    update = jnp.dot(rows, w_out[...], preferred_element_type=jnp.float32)
    out[...] = (latents[...].astype(jnp.float32) + update).astype(jnp.bfloat16)


def call(kernel, name, shapes, *operands, scalars=0, scratch=(), flops=0, moved=0):
    specs = [pl.BlockSpec(memory_space=pltpu.SMEM)] * scalars
    specs += [pl.BlockSpec(memory_space=pltpu.VMEM)] * (len(operands) - scalars)
    many = isinstance(shapes, (list, tuple))
    return pl.pallas_call(
        kernel,
        out_shape=shapes,
        in_specs=specs,
        out_specs=jax.tree.map(lambda _: pl.BlockSpec(memory_space=pltpu.VMEM), shapes)
        if many
        else pl.BlockSpec(memory_space=pltpu.VMEM),
        scratch_shapes=list(scratch),
        compiler_params=pltpu.CompilerParams(vmem_limit_bytes=VMEM),
        cost_estimate=pl.CostEstimate(flops=flops, bytes_accessed=moved, transcendentals=0),
        name=name,
    )(*operands)


def body(latents, norm_gain, w_query, w_key, w_value, w_out):
    _, positions, channels = latents.shape
    head = channels // HEADS
    own = latents[0]
    gain = norm_gain[None]
    frames = lax.axis_size("frame")
    frame = lax.axis_index("frame")
    row_count = lax.axis_size("row")
    total_positions = row_count * positions
    shape = lambda *dims, kind=jnp.bfloat16: jax.ShapeDtypeStruct(dims, kind)

    plan = spread_plan()
    flags = []
    for perms in plan:
        which = [0] * frames
        for k, pairs in enumerate(perms):
            for _, to in pairs:
                which[to] = k + 1
        flags.append(jnp.asarray(which, jnp.int32)[frame][None])

    held = own
    arrived = [lax.ppermute(held, "frame", pairs) for pairs in plan[0]]
    prior = lax.ppermute(own, "frame", [(i, i + 1) for i in range(frames - 1)])
    held = call(pick_kernel, "pick_a", shape(positions, channels), flags[0], held, *arrived, scalars=1)
    arrived = [lax.ppermute(held, "frame", pairs) for pairs in plan[1]]
    held = call(pick_kernel, "pick_b", shape(positions, channels), flags[1], held, *arrived, scalars=1)
    arrived = [lax.ppermute(held, "frame", pairs) for pairs in plan[2]]

    mine = call(
        own_kernel, "own_rows", shape(HEADS, 5 * head, positions),
        frame[None], own, prior, gain, w_query, w_key, w_value, scalars=1,
        flops=2 * positions * channels * channels * 5, moved=3 * 2 * channels * channels,
    )
    rows = lax.all_to_all(mine, "row", 0, 0, tiled=True)
    peak, total = call(
        near_kernel, "near", (shape(8, total_positions, kind=jnp.float32), shape(head + SPREAD, total_positions, kind=jnp.float32)),
        rows, flops=4 * head * total_positions * 2 * total_positions, moved=2 * 8 * 5 * head * positions,
    )
    theirs = call(
        first_kernel, "first_rows", shape(HEADS, 2 * head, positions),
        flags[2], held, *arrived, gain, w_key, w_value, scalars=1,
        scratch=[pltpu.VMEM((positions, channels), jnp.bfloat16)],
        flops=2 * positions * channels * channels * 2, moved=2 * 2 * channels * channels,
    )
    first = lax.all_to_all(theirs, "row", 0, 0, tiled=True)
    attended = call(
        far_kernel, "far", shape(HEADS, head, positions),
        rows, first, peak, total, flops=4 * head * total_positions * total_positions, moved=2 * 8 * 2 * head * positions,
    )
    back = lax.all_to_all(attended, "row", 0, 0, tiled=True)
    mixed = call(
        mix_kernel, "mix", shape(positions, channels),
        back, own, w_out, flops=2 * positions * channels * channels, moved=2 * channels * channels,
    )
    return mixed[None]


def solution(mesh):
    return jax.shard_map(
        body,
        mesh=mesh,
        in_specs=(P("frame", "row", None), P(), P(), P(), P(), P()),
        out_specs=P("frame", "row", None),
        check_vma=False,
    )
```

```python
import functools
import math

import jax
import jax.numpy as jnp
from jax import lax
from jax.experimental import pallas as pl
from jax.experimental.pallas import tpu as pltpu
from jax.sharding import PartitionSpec as P

HEADS = 8
SPREAD = 16
VMEM = 24 * 2**20
COST_A = 3 * 10**10
COST_B = 3 * 10**10

SIZES = (8, 4, 2)


def root(y, z, core):
    return (y == 0) & (z == 0) & (core == 0)


def lead(y, z, core):
    return (y % 2 == 0) & (z == 0) & (core == 0)


def wing(y, z, core):
    return (y % 2 == 0) & ((z != 0) ^ (core == 1))


def plain(y, z, core):
    return (y % 2 == 0) & (z != 0) & (core == 0)


ROUNDS = (
    ((root, (4, 0, 0)), (root, (2, 0, 0)), (root, (6, 0, 0))),
    ((lead, (0, 2, 0)), (lead, (0, 1, 0)), (lead, (0, 3, 0)), (lead, (0, 0, 1))),
    ((wing, (1, 0, 0)), (wing, (1, 0, 1)), (plain, (0, 0, 1))),
)


def place_of(frame):
    return frame // (SIZES[1] * SIZES[2]), frame // SIZES[2] % SIZES[1], frame % SIZES[2]


def pairs_of(senders, step):
    pairs = []
    for frame in range(math.prod(SIZES)):
        if senders(*place_of(frame)):
            y, z, core = ((a + b) % n for a, b, n in zip(place_of(frame), step, SIZES))
            pairs.append((frame, (y * SIZES[1] + z) * SIZES[2] + core))
    return pairs


def which_of(frame, turn):
    place = (frame >> 3, (frame >> 1) & 3, frame & 1)
    which = 0
    for k, (senders, step) in enumerate(ROUNDS[turn]):
        y, z, core = ((at - by) & (n - 1) for at, by, n in zip(place, step, SIZES))
        which = which + jnp.where(senders(y, z, core), k + 1, 0)
    return which


def normed_of(values, gain):
    values = values.astype(jnp.float32)
    center = values - jnp.mean(values, axis=-1, keepdims=True)
    spread = jnp.mean(center * center, axis=-1, keepdims=True)
    return (center * lax.rsqrt(spread + 1e-05) * gain).astype(jnp.bfloat16)


def project(normed, weight):
    return jnp.dot(normed, weight, preferred_element_type=jnp.float32)


def by_head(rows):
    channels, positions = rows.shape[1], rows.shape[0]
    return rows.astype(jnp.bfloat16).T.reshape(HEADS, channels // HEADS, positions)


def own_kernel(frame, own, prior, gain, w_query, w_key, w_value, after, out):
    del after
    positions, channels = own.shape
    head = channels // HEADS
    scale = math.log2(math.e) / math.sqrt(head)
    before = jnp.where(frame[0] == 0, own[...].astype(jnp.float32), prior[...].astype(jnp.float32))
    normed = normed_of(own[...], gain[...])
    both = jnp.concatenate([normed, normed_of(before, gain[...])], axis=0)
    out[:, :head, :] = by_head(project(normed, w_query[...]) * scale)
    for k, weight in enumerate((w_key, w_value)):
        rows = project(both, weight[...])
        out[:, (1 + k) * head : (2 + k) * head, :] = by_head(rows[:positions])
        out[:, (3 + k) * head : (4 + k) * head, :] = by_head(rows[positions:])


def pick_kernel(turn, frame, held, *rest):
    *arrived, out = rest
    which = which_of(frame[0], turn)
    for k, ref in enumerate((held, *arrived)):

        @pl.when(which == k)
        def _():
            if turn == 0 and k == 0:
                pltpu.sync_copy(ref, out)
            else:
                out[...] = ref[...]


def first_kernel(frame, held, *rest):
    *arrived, gain, w_key, w_value, out, latents = rest
    pick_kernel(2, frame, held, *arrived, latents)
    head = latents.shape[1] // HEADS
    normed = normed_of(latents[...], gain[...])
    out[:, :head, :] = by_head(project(normed, w_key[...]))
    out[:, head:, :] = by_head(project(normed, w_value[...]))


def joined(ref, start, size, blocks):
    return jnp.concatenate([ref[b, start : start + size, :] for b in blocks], axis=1)


def ones_row(count):
    return (lax.broadcasted_iota(jnp.int32, (SPREAD, count), 0) == 0).astype(jnp.float32).astype(jnp.bfloat16)


def scores_of(key, query):
    return lax.dot_general(key, query, (((0,), (0,)), ((), ())), preferred_element_type=jnp.float32)


GROUP = 4


def near_kernel(rows, peak, total, queries):
    blocks, _, width = rows.shape
    head = rows.shape[1] // 5
    every = range(blocks)
    keys = [joined(rows, start * head, head, every) for start in (1, 3)]
    values = [
        jnp.concatenate([joined(rows, start * head, head, every), ones_row(blocks * width)], axis=0)
        for start in (2, 4)
    ]
    for g in range(0, blocks, GROUP):
        query = joined(rows, 0, head, range(g, g + GROUP))
        queries[:, g * width : (g + GROUP) * width] = query
        scores = [scores_of(key, query) for key in keys]
        top = jnp.maximum(*[jnp.max(s, axis=0, keepdims=True) for s in scores])
        span = slice(g * width, (g + GROUP) * width)
        peak[:, span] = jnp.broadcast_to(top, (8, GROUP * width))
        total[:, span] = sum(
            jnp.dot(value, jnp.exp2(s - top).astype(jnp.bfloat16), preferred_element_type=jnp.float32)
            for value, s in zip(values, scores)
        )


def far_kernel(queries, first, peak, total, out):
    blocks, _, width = first.shape
    head = queries.shape[0]
    every = range(blocks)
    key = joined(first, 0, head, every)
    value = jnp.concatenate([joined(first, head, head, every), ones_row(blocks * width)], axis=0)
    for g in range(0, blocks, GROUP):
        span = slice(g * width, (g + GROUP) * width)
        scores = scores_of(key, queries[:, span])
        before = peak[:1, span]
        top = jnp.maximum(jnp.max(scores, axis=0, keepdims=True), before)
        weights = jnp.exp2(scores - top).astype(jnp.bfloat16)
        both = total[:, span] * jnp.exp2(before - top) + jnp.dot(
            value, weights, preferred_element_type=jnp.float32
        )
        attended = (both[:head] / both[head : head + 1]).astype(jnp.bfloat16)
        for b in range(GROUP):
            out[g + b] = attended[:, b * width : (b + 1) * width]


def mix_kernel(attended, latents, w_out, out):
    heads, head, positions = attended.shape
    rows = attended[...].reshape(heads * head, positions).T
    update = jnp.dot(rows, w_out[...], preferred_element_type=jnp.float32)
    out[...] = (latents[...].astype(jnp.float32) + update).astype(jnp.bfloat16)


def call(kernel, name, shapes, operands, kinds, scratch=(), flops=0, moved=0):
    spaces = {"s": pltpu.SMEM, "v": pltpu.VMEM, "a": pl.ANY}
    return pl.pallas_call(
        kernel,
        out_shape=shapes,
        in_specs=[pl.BlockSpec(memory_space=spaces[kind]) for kind in kinds],
        out_specs=jax.tree.map(lambda _: pl.BlockSpec(memory_space=pltpu.VMEM), shapes),
        scratch_shapes=list(scratch),
        compiler_params=pltpu.CompilerParams(vmem_limit_bytes=VMEM),
        cost_estimate=pl.CostEstimate(flops=int(flops), bytes_accessed=int(moved), transcendentals=0),
        name=name,
    )(*operands)


def body(latents, norm_gain, w_query, w_key, w_value, w_out):
    _, positions, channels = latents.shape
    head = channels // HEADS
    own = latents[0]
    frames = lax.axis_size("frame")
    at = lax.axis_index("frame")[None]
    total_positions = lax.axis_size("row") * positions

    def shape(*dims, kind=jnp.bfloat16):
        return jax.ShapeDtypeStruct(dims, kind)

    def send(array, turn):
        return [lax.ppermute(array, "frame", pairs_of(*permute)) for permute in ROUNDS[turn]]

    arrived = send(own, 0)
    prior = lax.ppermute(own, "frame", [(i, i + 1) for i in range(frames - 1)])
    held_a = call(
        functools.partial(pick_kernel, 0), "pick_a", shape(positions, channels),
        (at, own, *arrived), "savvv", flops=COST_A,
    )
    arrived = send(held_a, 1)
    held_b = call(
        functools.partial(pick_kernel, 1), "pick_b", shape(positions, channels),
        (at, held_a, *arrived), "svvvvv", flops=COST_B,
    )
    arrived = send(held_b, 2)

    mine = call(
        own_kernel, "own_rows", shape(HEADS, 5 * head, positions),
        (at, own, prior, norm_gain, w_query, w_key, w_value, held_a), "svvvvvva",
        flops=2 * positions * channels * channels * 5, moved=3 * 2 * channels * channels,
    )
    rows = lax.all_to_all(mine, "row", 0, 0, tiled=True)
    wide = (shape(8, total_positions, kind=jnp.float32), shape(head + SPREAD, total_positions, kind=jnp.float32))
    peak, total, queries = call(
        near_kernel, "near", (*wide, shape(head, total_positions)), (rows,), "v",
        flops=8 * head * total_positions * total_positions, moved=2 * 8 * 5 * head * positions,
    )
    theirs = call(
        first_kernel, "first_rows", shape(HEADS, 2 * head, positions),
        (at, held_b, *arrived, norm_gain, w_key, w_value), "svvvvvvv",
        scratch=[pltpu.VMEM((positions, channels), jnp.bfloat16)],
        flops=2 * positions * channels * channels * 2, moved=2 * 2 * channels * channels,
    )
    first = lax.all_to_all(theirs, "row", 0, 0, tiled=True)
    attended = call(
        far_kernel, "far", shape(HEADS, head, positions), (queries, first, peak, total), "vvvv",
        flops=4 * head * total_positions * total_positions, moved=2 * 8 * 2 * head * positions,
    )
    back = lax.all_to_all(attended, "row", 0, 0, tiled=True)
    mixed = call(
        mix_kernel, "mix", shape(positions, channels), (back, own, w_out), "vvv",
        flops=2 * positions * channels * channels, moved=2 * channels * channels,
    )
    return mixed[None]


def solution(mesh):
    return jax.shard_map(
        body,
        mesh=mesh,
        in_specs=(P("frame", "row", None), P(), P(), P(), P(), P()),
        out_specs=P("frame", "row", None),
        check_vma=False,
    )
```

```python
import functools
import math

import jax
import jax.numpy as jnp
from jax import lax
from jax.experimental import pallas as pl
from jax.experimental.pallas import tpu as pltpu
from jax.sharding import PartitionSpec as P

HEADS = 8
SPREAD = 16
VMEM = 24 * 2**20
COST_STAGE = 10**9
COST_A = 3 * 10**10
COST_B = 3 * 10**10

SIZES = (8, 4, 2)


def root(y, z, core):
    return (y == 0) & (z == 0) & (core == 0)


def lead(y, z, core):
    return (y % 2 == 0) & (z == 0) & (core == 0)


def even(y, z, core):
    return (y % 2 == 0) & (core == 0)


ROUNDS = (
    ((root, (4, 0, 0)), (root, (2, 0, 0)), (root, (6, 0, 0))),
    ((lead, (0, 1, 0)), (lead, (0, 2, 0)), (lead, (0, 3, 0))),
    ((even, (1, 0, 0)), (even, (1, 0, 1)), (even, (0, 0, 1))),
)


def place_of(frame):
    return frame // (SIZES[1] * SIZES[2]), frame // SIZES[2] % SIZES[1], frame % SIZES[2]


def pairs_of(senders, step):
    pairs = []
    for frame in range(math.prod(SIZES)):
        if senders(*place_of(frame)):
            y, z, core = ((a + b) % n for a, b, n in zip(place_of(frame), step, SIZES))
            pairs.append((frame, (y * SIZES[1] + z) * SIZES[2] + core))
    return pairs


def which_of(frame, turn):
    place = (frame >> 3, (frame >> 1) & 3, frame & 1)
    which = 0
    for k, (senders, step) in enumerate(ROUNDS[turn]):
        y, z, core = ((at - by) & (n - 1) for at, by, n in zip(place, step, SIZES))
        which = which + jnp.where(senders(y, z, core), k + 1, 0)
    return which


def normed_of(values, gain):
    values = values.astype(jnp.float32)
    center = values - jnp.mean(values, axis=-1, keepdims=True)
    spread = jnp.mean(center * center, axis=-1, keepdims=True)
    return (center * lax.rsqrt(spread + 1e-05) * gain).astype(jnp.bfloat16)


def project(normed, weight):
    return jnp.dot(normed, weight, preferred_element_type=jnp.float32)


def by_head(rows):
    channels, positions = rows.shape[1], rows.shape[0]
    return rows.astype(jnp.bfloat16).T.reshape(HEADS, channels // HEADS, positions)


def own_kernel(own, gain, w_query, w_key, w_value, out):
    head = own.shape[1] // HEADS
    normed = normed_of(own[...], gain[...])
    scale = math.log2(math.e) / math.sqrt(head)
    out[:, :head, :] = by_head(project(normed, w_query[...]) * scale)
    out[:, head : 2 * head, :] = by_head(project(normed, w_key[...]))
    out[:, 2 * head :, :] = by_head(project(normed, w_value[...]))


def prior_kernel(frame, mine, own, prior, gain, w_key, w_value, after, out, rows, done):
    del after
    head = own.shape[1] // HEADS
    copies = [pltpu.make_async_copy(mine, out.at[:, : 3 * head, :], done.at[2])]
    copies[0].start()
    before = jnp.where(frame[0] == 0, own[...].astype(jnp.float32), prior[...].astype(jnp.float32))
    normed = normed_of(before, gain[...])
    for k, weight in enumerate((w_key, w_value)):
        rows[k] = by_head(project(normed, weight[...]))
        copy = pltpu.make_async_copy(rows.at[k], out.at[:, (3 + k) * head : (4 + k) * head, :], done.at[k])
        copy.start()
        copies.append(copy)
    for copy in copies:
        copy.wait()


def stage_kernel(latents, out):
    pltpu.sync_copy(latents, out)


def pick_kernel(turn, frame, held, *rest):
    *arrived, out = rest
    which = which_of(frame[0], turn)
    for k, ref in enumerate((held, *arrived)):

        @pl.when(which == k)
        def _():
            out[...] = ref[...]


def first_kernel(frame, held, *rest):
    *arrived, gain, w_key, w_value, out, latents = rest
    pick_kernel(2, frame, held, *arrived, latents)
    head = latents.shape[1] // HEADS
    normed = normed_of(latents[...], gain[...])
    out[:, :head, :] = by_head(project(normed, w_key[...]))
    out[:, head:, :] = by_head(project(normed, w_value[...]))


def joined(ref, start, size, blocks):
    return jnp.concatenate([ref[b, start : start + size, :] for b in blocks], axis=1)


def ones_row(count):
    return (lax.broadcasted_iota(jnp.int32, (SPREAD, count), 0) == 0).astype(jnp.float32).astype(jnp.bfloat16)


def scores_of(key, query):
    return lax.dot_general(key, query, (((0,), (0,)), ((), ())), preferred_element_type=jnp.float32)


GROUP = 4


def near_kernel(rows, peak, total, queries):
    blocks, _, width = rows.shape
    head = rows.shape[1] // 5
    every = range(blocks)
    keys = [joined(rows, start * head, head, every) for start in (1, 3)]
    values = [
        jnp.concatenate([joined(rows, start * head, head, every), ones_row(blocks * width)], axis=0)
        for start in (2, 4)
    ]
    for g in range(0, blocks, GROUP):
        query = joined(rows, 0, head, range(g, g + GROUP))
        queries[:, g * width : (g + GROUP) * width] = query
        scores = [scores_of(key, query) for key in keys]
        top = jnp.maximum(*[jnp.max(s, axis=0, keepdims=True) for s in scores])
        span = slice(g * width, (g + GROUP) * width)
        peak[:, span] = jnp.broadcast_to(top, (8, GROUP * width))
        total[:, span] = sum(
            jnp.dot(value, jnp.exp2(s - top).astype(jnp.bfloat16), preferred_element_type=jnp.float32)
            for value, s in zip(values, scores)
        )


def far_kernel(queries, first, peak, total, out):
    blocks, _, width = first.shape
    head = queries.shape[0]
    every = range(blocks)
    value = jnp.concatenate([joined(first, head, head, every), ones_row(blocks * width)], axis=0)
    scores = scores_of(joined(first, 0, head, every), queries[...])
    before = peak[:1, :]
    top = jnp.maximum(jnp.max(scores, axis=0, keepdims=True), before)
    weights = jnp.exp2(scores - top).astype(jnp.bfloat16)
    both = total[...] * jnp.exp2(before - top) + jnp.dot(value, weights, preferred_element_type=jnp.float32)
    attended = (both[:head] / both[head : head + 1]).astype(jnp.bfloat16)
    for b in every:
        out[b] = attended[:, b * width : (b + 1) * width]


def mix_kernel(attended, latents, w_out, out):
    heads, head, positions = attended.shape
    rows = attended[...].reshape(heads * head, positions).T
    update = jnp.dot(rows, w_out[...], preferred_element_type=jnp.float32)
    out[...] = (latents[...].astype(jnp.float32) + update).astype(jnp.bfloat16)


def call(kernel, name, shapes, operands, kinds, to=pltpu.VMEM, scratch=(), flops=0, moved=0):
    spaces = {"s": pltpu.SMEM, "v": pltpu.VMEM, "a": pl.ANY}
    return pl.pallas_call(
        kernel,
        out_shape=shapes,
        in_specs=[pl.BlockSpec(memory_space=spaces[kind]) for kind in kinds],
        out_specs=jax.tree.map(lambda _: pl.BlockSpec(memory_space=to), shapes),
        scratch_shapes=list(scratch),
        compiler_params=pltpu.CompilerParams(vmem_limit_bytes=VMEM),
        cost_estimate=pl.CostEstimate(flops=int(flops), bytes_accessed=int(moved), transcendentals=0),
        name=name,
    )(*operands)


def body(latents, norm_gain, w_query, w_key, w_value, w_out):
    _, positions, channels = latents.shape
    head = channels // HEADS
    own = latents[0]
    frames = lax.axis_size("frame")
    at = lax.axis_index("frame")[None]
    total_positions = lax.axis_size("row") * positions

    def shape(*dims, kind=jnp.bfloat16):
        return jax.ShapeDtypeStruct(dims, kind)

    def send(array, turn):
        return [lax.ppermute(array, "frame", pairs_of(*permute)) for permute in ROUNDS[turn]]

    arrived = send(own, 0)
    prior = lax.ppermute(own, "frame", [(i, i + 1) for i in range(frames - 1)])
    own = call(stage_kernel, "stage", shape(positions, channels), (own,), "a", flops=COST_STAGE)
    held_a = call(
        functools.partial(pick_kernel, 0), "pick_a", shape(positions, channels),
        (at, own, *arrived), "svvvv", flops=COST_A,
    )
    arrived = send(held_a, 1)
    held_b = call(
        functools.partial(pick_kernel, 1), "pick_b", shape(positions, channels),
        (at, held_a, *arrived), "svvvv", flops=COST_B,
    )
    arrived = send(held_b, 2)

    mine = call(
        own_kernel, "own_rows", shape(HEADS, 3 * head, positions),
        (own, norm_gain, w_query, w_key, w_value), "vvvvv",
        flops=2 * positions * channels * channels * 3, moved=3 * 2 * channels * channels,
    )
    mine = call(
        prior_kernel, "prior_rows", shape(HEADS, 5 * head, positions),
        (at, mine, own, prior, norm_gain, w_key, w_value, held_a), "svvvvvva", to=pl.ANY,
        scratch=[pltpu.VMEM((2, HEADS, head, positions), jnp.bfloat16), pltpu.SemaphoreType.DMA((3,))],
        flops=2 * positions * channels * channels * 2, moved=2 * 2 * channels * channels,
    )
    rows = lax.all_to_all(mine, "row", 0, 0, tiled=True)
    wide = (shape(8, total_positions, kind=jnp.float32), shape(head + SPREAD, total_positions, kind=jnp.float32))
    peak, total, queries = call(
        near_kernel, "near", (*wide, shape(head, total_positions)), (rows,), "v",
        flops=8 * head * total_positions * total_positions, moved=2 * 8 * 5 * head * positions,
    )
    theirs = call(
        first_kernel, "first_rows", shape(HEADS, 2 * head, positions),
        (at, held_b, *arrived, norm_gain, w_key, w_value), "svvvvvvv",
        scratch=[pltpu.VMEM((positions, channels), jnp.bfloat16)],
        flops=2 * positions * channels * channels * 2, moved=2 * 2 * channels * channels,
    )
    first = lax.all_to_all(theirs, "row", 0, 0, tiled=True)
    attended = call(
        far_kernel, "far", shape(HEADS, head, positions), (queries, first, peak, total), "vvvv",
        flops=4 * head * total_positions * total_positions, moved=2 * 8 * 2 * head * positions,
    )
    back = lax.all_to_all(attended, "row", 0, 0, tiled=True)
    mixed = call(
        mix_kernel, "mix", shape(positions, channels), (back, own, w_out), "vvv",
        flops=2 * positions * channels * channels, moved=2 * channels * channels,
    )
    return mixed[None]


def solution(mesh):
    return jax.shard_map(
        body,
        mesh=mesh,
        in_specs=(P("frame", "row", None), P(), P(), P(), P(), P()),
        out_specs=P("frame", "row", None),
        check_vma=False,
    )
```

```python
import functools
import math

import jax
import jax.numpy as jnp
from jax import lax
from jax.experimental import pallas as pl
from jax.experimental.pallas import tpu as pltpu
from jax.sharding import PartitionSpec as P

HEADS = 8
SPREAD = 16
VMEM = 24 * 2**20
COST_STAGE = 10**9
COST_A = 3 * 10**10
COST_B = 3 * 10**10

SIZES = (8, 4, 2)


def root(y, z, core):
    return (y == 0) & (z == 0) & (core == 0)


def lead(y, z, core):
    return (y % 2 == 0) & (z == 0) & (core == 0)


def even(y, z, core):
    return (y % 2 == 0) & (core == 0)


def upper(y, z, core):
    return even(y, z, core) & (z != 0)


ROUNDS = (
    ((root, (2, 0, 0)), (root, (4, 0, 0)), (root, (6, 0, 0))),
    ((lead, (1, 0, 0)), (lead, (0, 1, 0)), (lead, (0, 2, 0)), (lead, (0, 3, 0))),
    ((upper, (1, 0, 0)), (even, (1, 0, 1)), (even, (0, 0, 1))),
)


def place_of(frame):
    return frame // (SIZES[1] * SIZES[2]), frame // SIZES[2] % SIZES[1], frame % SIZES[2]


def pairs_of(senders, step):
    pairs = []
    for frame in range(math.prod(SIZES)):
        if senders(*place_of(frame)):
            y, z, core = ((a + b) % n for a, b, n in zip(place_of(frame), step, SIZES))
            pairs.append((frame, (y * SIZES[1] + z) * SIZES[2] + core))
    return pairs


def which_of(frame, turn):
    place = (frame >> 3, (frame >> 1) & 3, frame & 1)
    which = 0
    for k, (senders, step) in enumerate(ROUNDS[turn]):
        y, z, core = ((at - by) & (n - 1) for at, by, n in zip(place, step, SIZES))
        which = which + jnp.where(senders(y, z, core), k + 1, 0)
    return which


def normed_of(values, gain):
    values = values.astype(jnp.float32)
    center = values - jnp.mean(values, axis=-1, keepdims=True)
    spread = jnp.mean(center * center, axis=-1, keepdims=True)
    return (center * lax.rsqrt(spread + 1e-05) * gain).astype(jnp.bfloat16)


def project(normed, weight):
    return jnp.dot(normed, weight, preferred_element_type=jnp.float32)


def by_head(rows):
    channels, positions = rows.shape[1], rows.shape[0]
    return rows.astype(jnp.bfloat16).T.reshape(HEADS, channels // HEADS, positions)


def own_kernel(own, gain, w_query, w_key, w_value, out):
    head = own.shape[1] // HEADS
    normed = normed_of(own[...], gain[...])
    scale = math.log2(math.e) / math.sqrt(head)
    out[:, :head, :] = by_head(project(normed, w_query[...]) * scale)
    out[:, head : 2 * head, :] = by_head(project(normed, w_key[...]))
    out[:, 2 * head :, :] = by_head(project(normed, w_value[...]))


def prior_kernel(frame, mine, own, prior, gain, w_key, w_value, after, out, rows, done):
    del after
    head = own.shape[1] // HEADS
    copies = [pltpu.make_async_copy(mine, out.at[:, : 3 * head, :], done.at[2])]
    copies[0].start()
    before = jnp.where(frame[0] == 0, own[...].astype(jnp.float32), prior[...].astype(jnp.float32))
    normed = normed_of(before, gain[...])
    for k, weight in enumerate((w_key, w_value)):
        rows[k] = by_head(project(normed, weight[...]))
        copy = pltpu.make_async_copy(rows.at[k], out.at[:, (3 + k) * head : (4 + k) * head, :], done.at[k])
        copy.start()
        copies.append(copy)
    for copy in copies:
        copy.wait()


def stage_kernel(latents, out):
    pltpu.sync_copy(latents, out)


def pick_kernel(turn, frame, held, *rest):
    *arrived, out = rest
    which = which_of(frame[0], turn)
    for k, ref in enumerate((held, *arrived)):

        @pl.when(which == k)
        def _():
            out[...] = ref[...]


def first_kernel(frame, held, *rest):
    *arrived, gain, w_key, w_value, out, latents = rest
    pick_kernel(2, frame, held, *arrived, latents)
    head = latents.shape[1] // HEADS
    normed = normed_of(latents[...], gain[...])
    out[:, :head, :] = by_head(project(normed, w_key[...]))
    out[:, head:, :] = by_head(project(normed, w_value[...]))


def joined(ref, start, size, blocks):
    return jnp.concatenate([ref[b, start : start + size, :] for b in blocks], axis=1)


def ones_row(count):
    return (lax.broadcasted_iota(jnp.int32, (SPREAD, count), 0) == 0).astype(jnp.float32).astype(jnp.bfloat16)


def scores_of(key, query):
    return lax.dot_general(key, query, (((0,), (0,)), ((), ())), preferred_element_type=jnp.float32)


GROUP = 4


def near_kernel(rows, peak, total, queries):
    blocks, _, width = rows.shape
    head = rows.shape[1] // 5
    every = range(blocks)
    keys = [joined(rows, start * head, head, every) for start in (1, 3)]
    values = [
        jnp.concatenate([joined(rows, start * head, head, every), ones_row(blocks * width)], axis=0)
        for start in (2, 4)
    ]
    for g in range(0, blocks, GROUP):
        query = joined(rows, 0, head, range(g, g + GROUP))
        queries[:, g * width : (g + GROUP) * width] = query
        scores = [scores_of(key, query) for key in keys]
        top = jnp.maximum(*[jnp.max(s, axis=0, keepdims=True) for s in scores])
        span = slice(g * width, (g + GROUP) * width)
        peak[:, span] = jnp.broadcast_to(top, (8, GROUP * width))
        total[:, span] = sum(
            jnp.dot(value, jnp.exp2(s - top).astype(jnp.bfloat16), preferred_element_type=jnp.float32)
            for value, s in zip(values, scores)
        )


def far_kernel(queries, first, peak, total, out):
    blocks, _, width = first.shape
    head = queries.shape[0]
    every = range(blocks)
    value = jnp.concatenate([joined(first, head, head, every), ones_row(blocks * width)], axis=0)
    scores = scores_of(joined(first, 0, head, every), queries[...])
    before = peak[:1, :]
    top = jnp.maximum(jnp.max(scores, axis=0, keepdims=True), before)
    weights = jnp.exp2(scores - top).astype(jnp.bfloat16)
    both = total[...] * jnp.exp2(before - top) + jnp.dot(value, weights, preferred_element_type=jnp.float32)
    attended = (both[:head] / both[head : head + 1]).astype(jnp.bfloat16)
    for b in every:
        out[b] = attended[:, b * width : (b + 1) * width]


def mix_kernel(attended, latents, w_out, out):
    heads, head, positions = attended.shape
    rows = attended[...].reshape(heads * head, positions).T
    update = jnp.dot(rows, w_out[...], preferred_element_type=jnp.float32)
    out[...] = (latents[...].astype(jnp.float32) + update).astype(jnp.bfloat16)


def call(kernel, name, shapes, operands, kinds, to=pltpu.VMEM, scratch=(), flops=0, moved=0):
    spaces = {"s": pltpu.SMEM, "v": pltpu.VMEM, "a": pl.ANY}
    return pl.pallas_call(
        kernel,
        out_shape=shapes,
        in_specs=[pl.BlockSpec(memory_space=spaces[kind]) for kind in kinds],
        out_specs=jax.tree.map(lambda _: pl.BlockSpec(memory_space=to), shapes),
        scratch_shapes=list(scratch),
        compiler_params=pltpu.CompilerParams(vmem_limit_bytes=VMEM),
        cost_estimate=pl.CostEstimate(flops=int(flops), bytes_accessed=int(moved), transcendentals=0),
        name=name,
    )(*operands)


def body(latents, norm_gain, w_query, w_key, w_value, w_out):
    _, positions, channels = latents.shape
    head = channels // HEADS
    own = latents[0]
    frames = lax.axis_size("frame")
    at = lax.axis_index("frame")[None]
    total_positions = lax.axis_size("row") * positions

    def shape(*dims, kind=jnp.bfloat16):
        return jax.ShapeDtypeStruct(dims, kind)

    def send(array, turn):
        return [lax.ppermute(array, "frame", pairs_of(*permute)) for permute in ROUNDS[turn]]

    arrived = send(own, 0)
    prior = lax.ppermute(own, "frame", [(i, i + 1) for i in range(frames - 1)])
    own = call(stage_kernel, "stage", shape(positions, channels), (own,), "a", flops=COST_STAGE)
    held_a = call(
        functools.partial(pick_kernel, 0), "pick_a", shape(positions, channels),
        (at, own, *arrived), "svvvv", flops=COST_A,
    )
    arrived = send(held_a, 1)
    held_b = call(
        functools.partial(pick_kernel, 1), "pick_b", shape(positions, channels),
        (at, held_a, *arrived), "svvvvv", flops=COST_B,
    )
    arrived = send(held_b, 2)

    mine = call(
        own_kernel, "own_rows", shape(HEADS, 3 * head, positions),
        (own, norm_gain, w_query, w_key, w_value), "vvvvv",
        flops=2 * positions * channels * channels * 3, moved=3 * 2 * channels * channels,
    )
    mine = call(
        prior_kernel, "prior_rows", shape(HEADS, 5 * head, positions),
        (at, mine, own, prior, norm_gain, w_key, w_value, held_a), "svvvvvva", to=pl.ANY,
        scratch=[pltpu.VMEM((2, HEADS, head, positions), jnp.bfloat16), pltpu.SemaphoreType.DMA((3,))],
        flops=2 * positions * channels * channels * 2, moved=2 * 2 * channels * channels,
    )
    rows = lax.all_to_all(mine, "row", 0, 0, tiled=True)
    wide = (shape(8, total_positions, kind=jnp.float32), shape(head + SPREAD, total_positions, kind=jnp.float32))
    peak, total, queries = call(
        near_kernel, "near", (*wide, shape(head, total_positions)), (rows,), "v",
        flops=8 * head * total_positions * total_positions, moved=2 * 8 * 5 * head * positions,
    )
    theirs = call(
        first_kernel, "first_rows", shape(HEADS, 2 * head, positions),
        (at, held_b, *arrived, norm_gain, w_key, w_value), "svvvvvvv",
        scratch=[pltpu.VMEM((positions, channels), jnp.bfloat16)],
        flops=2 * positions * channels * channels * 2, moved=2 * 2 * channels * channels,
    )
    first = lax.all_to_all(theirs, "row", 0, 0, tiled=True)
    attended = call(
        far_kernel, "far", shape(HEADS, head, positions), (queries, first, peak, total), "vvvv",
        flops=4 * head * total_positions * total_positions, moved=2 * 8 * 2 * head * positions,
    )
    back = lax.all_to_all(attended, "row", 0, 0, tiled=True)
    mixed = call(
        mix_kernel, "mix", shape(positions, channels), (back, own, w_out), "vvv",
        flops=2 * positions * channels * channels, moved=2 * channels * channels,
    )
    return mixed[None]


def solution(mesh):
    return jax.shard_map(
        body,
        mesh=mesh,
        in_specs=(P("frame", "row", None), P(), P(), P(), P(), P()),
        out_specs=P("frame", "row", None),
        check_vma=False,
    )
```

```python
import functools
import math

import jax
import jax.numpy as jnp
from jax import lax
from jax.experimental import pallas as pl
from jax.experimental.pallas import tpu as pltpu
from jax.sharding import PartitionSpec as P

HEADS = 8
SPREAD = 16
VMEM = 24 * 2**20
COST_STAGE = 10**9
COST_A = 3 * 10**10
COST_B = 3 * 10**10

SIZES = (8, 4, 2)


def root(y, z, core):
    return (y == 0) & (z == 0) & (core == 0)


def lead(y, z, core):
    return (y % 2 == 0) & (z == 0) & (core == 0)


def even(y, z, core):
    return (y % 2 == 0) & (core == 0)


def upper(y, z, core):
    return even(y, z, core) & (z != 0)


ROUNDS = (
    ((root, (2, 0, 0)), (root, (4, 0, 0)), (root, (6, 0, 0))),
    ((lead, (1, 0, 0)), (lead, (0, 1, 0)), (lead, (0, 2, 0)), (lead, (0, 3, 0))),
    ((upper, (1, 0, 0)), (even, (1, 0, 1)), (even, (0, 0, 1))),
)


def place_of(frame):
    return frame // (SIZES[1] * SIZES[2]), frame // SIZES[2] % SIZES[1], frame % SIZES[2]


def pairs_of(senders, step):
    pairs = []
    for frame in range(math.prod(SIZES)):
        if senders(*place_of(frame)):
            y, z, core = ((a + b) % n for a, b, n in zip(place_of(frame), step, SIZES))
            pairs.append((frame, (y * SIZES[1] + z) * SIZES[2] + core))
    return pairs


def which_of(frame, turn):
    place = (frame >> 3, (frame >> 1) & 3, frame & 1)
    which = 0
    for k, (senders, step) in enumerate(ROUNDS[turn]):
        y, z, core = ((at - by) & (n - 1) for at, by, n in zip(place, step, SIZES))
        which = which + jnp.where(senders(y, z, core), k + 1, 0)
    return which


def normed_of(values, gain):
    values = values.astype(jnp.float32)
    center = values - jnp.mean(values, axis=-1, keepdims=True)
    spread = jnp.mean(center * center, axis=-1, keepdims=True)
    return (center * lax.rsqrt(spread + 1e-05) * gain).astype(jnp.bfloat16)


def project(normed, weight):
    return jnp.dot(normed, weight, preferred_element_type=jnp.float32)


def by_head(rows):
    channels, positions = rows.shape[1], rows.shape[0]
    return rows.astype(jnp.bfloat16).T.reshape(HEADS, channels // HEADS, positions)


def own_kernel(own, gain, w_query, w_key, w_value, out):
    head = own.shape[1] // HEADS
    normed = normed_of(own[...], gain[...])
    scale = math.log2(math.e) / math.sqrt(head)
    out[:, :head, :] = by_head(project(normed, w_query[...]) * scale)
    out[:, head : 2 * head, :] = by_head(project(normed, w_key[...]))
    out[:, 2 * head :, :] = by_head(project(normed, w_value[...]))


def prior_kernel(frame, mine, own, prior, gain, w_key, w_value, after, out, rows, done):
    del after
    head = own.shape[1] // HEADS
    copies = [pltpu.make_async_copy(mine, out.at[:, : 3 * head, :], done.at[2])]
    copies[0].start()
    before = jnp.where(frame[0] == 0, own[...].astype(jnp.float32), prior[...].astype(jnp.float32))
    normed = normed_of(before, gain[...])
    for k, weight in enumerate((w_key, w_value)):
        rows[k] = by_head(project(normed, weight[...]))
        copy = pltpu.make_async_copy(rows.at[k], out.at[:, (3 + k) * head : (4 + k) * head, :], done.at[k])
        copy.start()
        copies.append(copy)
    for copy in copies:
        copy.wait()


def stage_kernel(latents, out):
    pltpu.sync_copy(latents, out)


def pick_kernel(turn, frame, held, *rest):
    *arrived, out = rest
    which = which_of(frame[0], turn)
    for k, ref in enumerate((held, *arrived)):

        @pl.when(which == k)
        def _():
            out[...] = ref[...]


def first_kernel(frame, held, *rest):
    *arrived, gain, w_key, w_value, out, latents = rest
    pick_kernel(2, frame, held, *arrived, latents)
    head = latents.shape[1] // HEADS
    normed = normed_of(latents[...], gain[...])
    out[:, :head, :] = by_head(project(normed, w_key[...]))
    out[:, head:, :] = by_head(project(normed, w_value[...]))


def joined(ref, start, size, blocks):
    return jnp.concatenate([ref[b, start : start + size, :] for b in blocks], axis=1)


def ones_row(count):
    return (lax.broadcasted_iota(jnp.int32, (SPREAD, count), 0) == 0).astype(jnp.float32).astype(jnp.bfloat16)


def scores_of(key, query):
    return lax.dot_general(key, query, (((0,), (0,)), ((), ())), preferred_element_type=jnp.float32)


GROUP = 4


def near_kernel(rows, peak, total, queries):
    blocks, _, width = rows.shape
    head = rows.shape[1] // 5
    every = range(blocks)
    keys = [joined(rows, start * head, head, every) for start in (1, 3)]
    values = [
        jnp.concatenate([joined(rows, start * head, head, every), ones_row(blocks * width)], axis=0)
        for start in (2, 4)
    ]
    for g in range(0, blocks, GROUP):
        query = joined(rows, 0, head, range(g, g + GROUP))
        queries[:, g * width : (g + GROUP) * width] = query
        scores = [scores_of(key, query) for key in keys]
        top = jnp.maximum(*[jnp.max(s, axis=0, keepdims=True) for s in scores])
        span = slice(g * width, (g + GROUP) * width)
        peak[:, span] = jnp.broadcast_to(top, (8, GROUP * width))
        total[:, span] = sum(
            jnp.dot(value, jnp.exp2(s - top).astype(jnp.bfloat16), preferred_element_type=jnp.float32)
            for value, s in zip(values, scores)
        )


FAR = 60.0


def far_kernel(queries, first, peak, total, out, sums):
    blocks, _, width = first.shape
    head = queries.shape[0]
    every = range(blocks)
    key = joined(first, 0, head, every)
    value = jnp.concatenate([joined(first, head, head, every), ones_row(blocks * width)], axis=0)
    before = peak[:1, :]

    def weighted(scores, top):
        weights = jnp.exp2(scores - top).astype(jnp.bfloat16)
        return jnp.dot(value, weights, preferred_element_type=jnp.float32)

    scores = scores_of(key, queries[...])
    top = jnp.max(scores, axis=0, keepdims=True)
    sums[...] = total[...] + weighted(scores, before)

    @pl.when(jnp.max(top - before) > FAR)
    def _():
        both = jnp.maximum(top, before)
        sums[...] = total[...] * jnp.exp2(before - both) + weighted(scores_of(key, queries[...]), both)

    attended = (sums[:head, :] * (1.0 / sums[head : head + 1, :])).astype(jnp.bfloat16)
    for b in every:
        out[b] = attended[:, b * width : (b + 1) * width]


def mix_kernel(attended, latents, w_out, out):
    heads, head, positions = attended.shape
    rows = attended[...].reshape(heads * head, positions).T
    update = jnp.dot(rows, w_out[...], preferred_element_type=jnp.float32)
    out[...] = (latents[...].astype(jnp.float32) + update).astype(jnp.bfloat16)


def call(kernel, name, shapes, operands, kinds, to=pltpu.VMEM, scratch=(), flops=0, moved=0):
    spaces = {"s": pltpu.SMEM, "v": pltpu.VMEM, "a": pl.ANY}
    return pl.pallas_call(
        kernel,
        out_shape=shapes,
        in_specs=[pl.BlockSpec(memory_space=spaces[kind]) for kind in kinds],
        out_specs=jax.tree.map(lambda _: pl.BlockSpec(memory_space=to), shapes),
        scratch_shapes=list(scratch),
        compiler_params=pltpu.CompilerParams(vmem_limit_bytes=VMEM),
        cost_estimate=pl.CostEstimate(flops=int(flops), bytes_accessed=int(moved), transcendentals=0),
        name=name,
    )(*operands)


def body(latents, norm_gain, w_query, w_key, w_value, w_out):
    _, positions, channels = latents.shape
    head = channels // HEADS
    own = latents[0]
    frames = lax.axis_size("frame")
    at = lax.axis_index("frame")[None]
    total_positions = lax.axis_size("row") * positions

    def shape(*dims, kind=jnp.bfloat16):
        return jax.ShapeDtypeStruct(dims, kind)

    def send(array, turn):
        return [lax.ppermute(array, "frame", pairs_of(*permute)) for permute in ROUNDS[turn]]

    arrived = send(own, 0)
    prior = lax.ppermute(own, "frame", [(i, i + 1) for i in range(frames - 1)])
    own = call(stage_kernel, "stage", shape(positions, channels), (own,), "a", flops=COST_STAGE)
    held_a = call(
        functools.partial(pick_kernel, 0), "pick_a", shape(positions, channels),
        (at, own, *arrived), "svvvv", flops=COST_A,
    )
    arrived = send(held_a, 1)
    held_b = call(
        functools.partial(pick_kernel, 1), "pick_b", shape(positions, channels),
        (at, held_a, *arrived), "svvvvv", flops=COST_B,
    )
    arrived = send(held_b, 2)

    mine = call(
        own_kernel, "own_rows", shape(HEADS, 3 * head, positions),
        (own, norm_gain, w_query, w_key, w_value), "vvvvv",
        flops=2 * positions * channels * channels * 3, moved=3 * 2 * channels * channels,
    )
    mine = call(
        prior_kernel, "prior_rows", shape(HEADS, 5 * head, positions),
        (at, mine, own, prior, norm_gain, w_key, w_value, held_a), "svvvvvva", to=pl.ANY,
        scratch=[pltpu.VMEM((2, HEADS, head, positions), jnp.bfloat16), pltpu.SemaphoreType.DMA((3,))],
        flops=2 * positions * channels * channels * 2, moved=2 * 2 * channels * channels,
    )
    rows = lax.all_to_all(mine, "row", 0, 0, tiled=True)
    wide = (shape(8, total_positions, kind=jnp.float32), shape(head + SPREAD, total_positions, kind=jnp.float32))
    peak, total, queries = call(
        near_kernel, "near", (*wide, shape(head, total_positions)), (rows,), "v",
        flops=8 * head * total_positions * total_positions, moved=2 * 8 * 5 * head * positions,
    )
    theirs = call(
        first_kernel, "first_rows", shape(HEADS, 2 * head, positions),
        (at, held_b, *arrived, norm_gain, w_key, w_value), "svvvvvvv",
        scratch=[pltpu.VMEM((positions, channels), jnp.bfloat16)],
        flops=2 * positions * channels * channels * 2, moved=2 * 2 * channels * channels,
    )
    first = lax.all_to_all(theirs, "row", 0, 0, tiled=True)
    attended = call(
        far_kernel, "far", shape(HEADS, head, positions), (queries, first, peak, total), "vvvv",
        scratch=[pltpu.VMEM((head + SPREAD, total_positions), jnp.float32)],
        flops=4 * head * total_positions * total_positions, moved=2 * 8 * 2 * head * positions,
    )
    back = lax.all_to_all(attended, "row", 0, 0, tiled=True)
    mixed = call(
        mix_kernel, "mix", shape(positions, channels), (back, own, w_out), "vvv",
        flops=2 * positions * channels * channels, moved=2 * channels * channels,
    )
    return mixed[None]


def solution(mesh):
    return jax.shard_map(
        body,
        mesh=mesh,
        in_specs=(P("frame", "row", None), P(), P(), P(), P(), P()),
        out_specs=P("frame", "row", None),
        check_vma=False,
    )
```

```python
import functools
import math

import jax
import jax.numpy as jnp
from jax import lax
from jax.experimental import pallas as pl
from jax.experimental.pallas import tpu as pltpu
from jax.sharding import PartitionSpec as P

HEADS = 8
SPREAD = 16
VMEM = 24 * 2**20
STAGE_VMEM = 62 * 2**20
COST_STAGE = 10**9
COST_A = 3 * 10**10
COST_B = 3 * 10**10

SIZES = (8, 4, 2)


def root(y, z, core):
    return (y == 0) & (z == 0) & (core == 0)


def lead(y, z, core):
    return (y % 2 == 0) & (z == 0) & (core == 0)


def even(y, z, core):
    return (y % 2 == 0) & (core == 0)


def upper(y, z, core):
    return even(y, z, core) & (z != 0)


ROUNDS = (
    ((root, (2, 0, 0)), (root, (4, 0, 0)), (root, (6, 0, 0))),
    ((lead, (1, 0, 0)), (lead, (0, 1, 0)), (lead, (0, 2, 0)), (lead, (0, 3, 0))),
    ((upper, (1, 0, 0)), (even, (1, 0, 1)), (even, (0, 0, 1))),
)


def place_of(frame):
    return frame // (SIZES[1] * SIZES[2]), frame // SIZES[2] % SIZES[1], frame % SIZES[2]


def pairs_of(senders, step):
    pairs = []
    for frame in range(math.prod(SIZES)):
        if senders(*place_of(frame)):
            y, z, core = ((a + b) % n for a, b, n in zip(place_of(frame), step, SIZES))
            pairs.append((frame, (y * SIZES[1] + z) * SIZES[2] + core))
    return pairs


def which_of(frame, turn):
    place = (frame >> 3, (frame >> 1) & 3, frame & 1)
    which = 0
    for k, (senders, step) in enumerate(ROUNDS[turn]):
        y, z, core = ((at - by) & (n - 1) for at, by, n in zip(place, step, SIZES))
        which = which + jnp.where(senders(y, z, core), k + 1, 0)
    return which


def normed_of(values, gain):
    values = values.astype(jnp.float32)
    center = values - jnp.mean(values, axis=-1, keepdims=True)
    spread = jnp.mean(center * center, axis=-1, keepdims=True)
    return (center * lax.rsqrt(spread + 1e-05) * gain).astype(jnp.bfloat16)


def project(normed, weight):
    return jnp.dot(normed, weight, preferred_element_type=jnp.float32)


def by_head(rows):
    channels, positions = rows.shape[1], rows.shape[0]
    return rows.astype(jnp.bfloat16).T.reshape(HEADS, channels // HEADS, positions)


def own_kernel(own, gain, w_query, w_key, w_value, out):
    head = own.shape[1] // HEADS
    normed = normed_of(own[...], gain[...])
    scale = math.log2(math.e) / math.sqrt(head)
    out[:, :head, :] = by_head(project(normed, w_query[...]) * scale)
    out[:, head : 2 * head, :] = by_head(project(normed, w_key[...]))
    out[:, 2 * head :, :] = by_head(project(normed, w_value[...]))


def prior_kernel(frame, mine, own, prior, gain, w_key, w_value, after, out, rows, done):
    del after
    head = own.shape[1] // HEADS
    copies = [pltpu.make_async_copy(mine, out.at[:, : 3 * head, :], done.at[2])]
    copies[0].start()
    before = jnp.where(frame[0] == 0, own[...].astype(jnp.float32), prior[...].astype(jnp.float32))
    normed = normed_of(before, gain[...])
    for k, weight in enumerate((w_key, w_value)):
        rows[k] = by_head(project(normed, weight[...]))
        copy = pltpu.make_async_copy(rows.at[k], out.at[:, (3 + k) * head : (4 + k) * head, :], done.at[k])
        copy.start()
        copies.append(copy)
    for copy in copies:
        copy.wait()


def stage_kernel(latents, out):
    pltpu.sync_copy(latents, out)


def pick_kernel(turn, frame, held, *rest):
    *arrived, out = rest
    which = which_of(frame[0], turn)
    for k, ref in enumerate((held, *arrived)):

        @pl.when(which == k)
        def _():
            out[...] = ref[...]


def first_kernel(frame, held, *rest):
    *arrived, gain, w_key, w_value, out, latents = rest
    pick_kernel(2, frame, held, *arrived, latents)
    head = latents.shape[1] // HEADS
    normed = normed_of(latents[...], gain[...])
    out[:, :head, :] = by_head(project(normed, w_key[...]))
    out[:, head:, :] = by_head(project(normed, w_value[...]))


def joined(ref, start, size, blocks):
    return jnp.concatenate([ref[b, start : start + size, :] for b in blocks], axis=1)


def ones_row(count):
    return (lax.broadcasted_iota(jnp.int32, (SPREAD, count), 0) == 0).astype(jnp.float32).astype(jnp.bfloat16)


def scores_of(key, query):
    return lax.dot_general(key, query, (((0,), (0,)), ((), ())), preferred_element_type=jnp.float32)


GROUP = 4


def near_kernel(rows, peak, total, queries):
    blocks, _, width = rows.shape
    head = rows.shape[1] // 5
    every = range(blocks)
    keys = [joined(rows, start * head, head, every) for start in (1, 3)]
    values = [
        jnp.concatenate([joined(rows, start * head, head, every), ones_row(blocks * width)], axis=0)
        for start in (2, 4)
    ]
    for g in range(0, blocks, GROUP):
        query = joined(rows, 0, head, range(g, g + GROUP))
        queries[:, g * width : (g + GROUP) * width] = query
        scores = [scores_of(key, query) for key in keys]
        top = jnp.maximum(*[jnp.max(s, axis=0, keepdims=True) for s in scores])
        span = slice(g * width, (g + GROUP) * width)
        peak[:, span] = jnp.broadcast_to(top, (8, GROUP * width))
        total[:, span] = sum(
            jnp.dot(value, jnp.exp2(s - top).astype(jnp.bfloat16), preferred_element_type=jnp.float32)
            for value, s in zip(values, scores)
        )


FAR = 60.0


def far_kernel(queries, first, peak, total, out, sums):
    blocks, _, width = first.shape
    head = queries.shape[0]
    every = range(blocks)
    key = joined(first, 0, head, every)
    value = jnp.concatenate([joined(first, head, head, every), ones_row(blocks * width)], axis=0)
    before = peak[:1, :]

    def weighted(scores, top):
        weights = jnp.exp2(scores - top).astype(jnp.bfloat16)
        return jnp.dot(value, weights, preferred_element_type=jnp.float32)

    scores = scores_of(key, queries[...])
    top = jnp.max(scores, axis=0, keepdims=True)
    sums[...] = total[...] + weighted(scores, before)

    @pl.when(jnp.max(top - before) > FAR)
    def _():
        both = jnp.maximum(top, before)
        sums[...] = total[...] * jnp.exp2(before - both) + weighted(scores_of(key, queries[...]), both)

    attended = (sums[:head, :] * (1.0 / sums[head : head + 1, :])).astype(jnp.bfloat16)
    for b in every:
        out[b] = attended[:, b * width : (b + 1) * width]


def mix_kernel(attended, latents, w_out, out):
    heads, head, positions = attended.shape
    rows = attended[...].reshape(heads * head, positions).T
    update = jnp.dot(rows, w_out[...], preferred_element_type=jnp.float32)
    out[...] = (latents[...].astype(jnp.float32) + update).astype(jnp.bfloat16)


def call(kernel, name, shapes, operands, kinds, to=pltpu.VMEM, scratch=(), vmem=VMEM, flops=0, moved=0):
    spaces = {"s": pltpu.SMEM, "v": pltpu.VMEM, "a": pl.ANY}
    return pl.pallas_call(
        kernel,
        out_shape=shapes,
        in_specs=[pl.BlockSpec(memory_space=spaces[kind]) for kind in kinds],
        out_specs=jax.tree.map(lambda _: pl.BlockSpec(memory_space=to), shapes),
        scratch_shapes=list(scratch),
        compiler_params=pltpu.CompilerParams(vmem_limit_bytes=vmem),
        cost_estimate=pl.CostEstimate(flops=int(flops), bytes_accessed=int(moved), transcendentals=0),
        name=name,
    )(*operands)


def body(latents, norm_gain, w_query, w_key, w_value, w_out):
    _, positions, channels = latents.shape
    head = channels // HEADS
    own = latents[0]
    frames = lax.axis_size("frame")
    at = lax.axis_index("frame")[None]
    total_positions = lax.axis_size("row") * positions

    def shape(*dims, kind=jnp.bfloat16):
        return jax.ShapeDtypeStruct(dims, kind)

    def send(array, turn):
        return [lax.ppermute(array, "frame", pairs_of(*permute)) for permute in ROUNDS[turn]]

    arrived = send(own, 0)
    prior = lax.ppermute(own, "frame", [(i, i + 1) for i in range(frames - 1)])
    own = call(stage_kernel, "stage", shape(positions, channels), (own,), "a", vmem=STAGE_VMEM, flops=COST_STAGE)
    held_a = call(
        functools.partial(pick_kernel, 0), "pick_a", shape(positions, channels),
        (at, own, *arrived), "svvvv", flops=COST_A,
    )
    arrived = send(held_a, 1)
    held_b = call(
        functools.partial(pick_kernel, 1), "pick_b", shape(positions, channels),
        (at, held_a, *arrived), "svvvvv", flops=COST_B,
    )
    arrived = send(held_b, 2)

    mine = call(
        own_kernel, "own_rows", shape(HEADS, 3 * head, positions),
        (own, norm_gain, w_query, w_key, w_value), "vvvvv",
        flops=2 * positions * channels * channels * 3, moved=3 * 2 * channels * channels,
    )
    mine = call(
        prior_kernel, "prior_rows", shape(HEADS, 5 * head, positions),
        (at, mine, own, prior, norm_gain, w_key, w_value, held_a), "svvvvvva", to=pl.ANY,
        scratch=[pltpu.VMEM((2, HEADS, head, positions), jnp.bfloat16), pltpu.SemaphoreType.DMA((3,))],
        flops=2 * positions * channels * channels * 2, moved=2 * 2 * channels * channels,
    )
    rows = lax.all_to_all(mine, "row", 0, 0, tiled=True)
    wide = (shape(8, total_positions, kind=jnp.float32), shape(head + SPREAD, total_positions, kind=jnp.float32))
    peak, total, queries = call(
        near_kernel, "near", (*wide, shape(head, total_positions)), (rows,), "v",
        flops=8 * head * total_positions * total_positions, moved=2 * 8 * 5 * head * positions,
    )
    theirs = call(
        first_kernel, "first_rows", shape(HEADS, 2 * head, positions),
        (at, held_b, *arrived, norm_gain, w_key, w_value), "svvvvvvv",
        scratch=[pltpu.VMEM((positions, channels), jnp.bfloat16)],
        flops=2 * positions * channels * channels * 2, moved=2 * 2 * channels * channels,
    )
    first = lax.all_to_all(theirs, "row", 0, 0, tiled=True)
    attended = call(
        far_kernel, "far", shape(HEADS, head, positions), (queries, first, peak, total), "vvvv",
        scratch=[pltpu.VMEM((head + SPREAD, total_positions), jnp.float32)],
        flops=4 * head * total_positions * total_positions, moved=2 * 8 * 2 * head * positions,
    )
    back = lax.all_to_all(attended, "row", 0, 0, tiled=True)
    mixed = call(
        mix_kernel, "mix", shape(positions, channels), (back, own, w_out), "vvv",
        flops=2 * positions * channels * channels, moved=2 * channels * channels,
    )
    return mixed[None]


def solution(mesh):
    return jax.shard_map(
        body,
        mesh=mesh,
        in_specs=(P("frame", "row", None), P(), P(), P(), P(), P()),
        out_specs=P("frame", "row", None),
        check_vma=False,
    )
```

```python
import functools
import math

import jax
import jax.numpy as jnp
from jax import lax
from jax.experimental import pallas as pl
from jax.experimental.pallas import tpu as pltpu
from jax.sharding import PartitionSpec as P

HEADS = 8
SPREAD = 16
VMEM = 24 * 2**20
COST_STAGE = 10**9
COST_A = 3 * 10**10
COST_B = 3 * 10**10

SIZES = (8, 4, 2)


def root(y, z, core):
    return (y == 0) & (z == 0) & (core == 0)


def lead(y, z, core):
    return (y % 2 == 0) & (z == 0) & (core == 0)


def even(y, z, core):
    return (y % 2 == 0) & (core == 0)


def upper(y, z, core):
    return even(y, z, core) & (z != 0)


ROUNDS = (
    ((root, (2, 0, 0)), (root, (4, 0, 0)), (root, (6, 0, 0))),
    ((lead, (1, 0, 0)), (lead, (0, 1, 0)), (lead, (0, 2, 0)), (lead, (0, 3, 0))),
    ((upper, (1, 0, 0)), (even, (1, 0, 1)), (even, (0, 0, 1))),
)


def place_of(frame):
    return frame // (SIZES[1] * SIZES[2]), frame // SIZES[2] % SIZES[1], frame % SIZES[2]


def pairs_of(senders, step):
    pairs = []
    for frame in range(math.prod(SIZES)):
        if senders(*place_of(frame)):
            y, z, core = ((a + b) % n for a, b, n in zip(place_of(frame), step, SIZES))
            pairs.append((frame, (y * SIZES[1] + z) * SIZES[2] + core))
    return pairs


def which_of(frame, turn):
    place = (frame >> 3, (frame >> 1) & 3, frame & 1)
    which = 0
    for k, (senders, step) in enumerate(ROUNDS[turn]):
        y, z, core = ((at - by) & (n - 1) for at, by, n in zip(place, step, SIZES))
        which = which + jnp.where(senders(y, z, core), k + 1, 0)
    return which


def normed_of(values, gain):
    values = values.astype(jnp.float32)
    center = values - jnp.mean(values, axis=-1, keepdims=True)
    spread = jnp.mean(center * center, axis=-1, keepdims=True)
    return (center * lax.rsqrt(spread + 1e-05) * gain).astype(jnp.bfloat16)


def project(normed, weight):
    return jnp.dot(normed, weight, preferred_element_type=jnp.float32)


def by_head(rows):
    channels, positions = rows.shape[1], rows.shape[0]
    return rows.astype(jnp.bfloat16).T.reshape(HEADS, channels // HEADS, positions)


def own_kernel(own, gain, w_query, w_key, w_value, out):
    head = own.shape[1] // HEADS
    normed = normed_of(own[...], gain[...])
    scale = math.log2(math.e) / math.sqrt(head)
    out[:, :head, :] = by_head(project(normed, w_query[...]) * scale)
    out[:, head : 2 * head, :] = by_head(project(normed, w_key[...]))
    out[:, 2 * head :, :] = by_head(project(normed, w_value[...]))


def prior_kernel(frame, mine, own, prior, gain, w_key, w_value, after, out, rows, done):
    del after
    head = own.shape[1] // HEADS
    copies = [pltpu.make_async_copy(mine, out.at[:, : 3 * head, :], done.at[2])]
    copies[0].start()
    before = jnp.where(frame[0] == 0, own[...].astype(jnp.float32), prior[...].astype(jnp.float32))
    normed = normed_of(before, gain[...])
    for k, weight in enumerate((w_key, w_value)):
        rows[k] = by_head(project(normed, weight[...]))
        copy = pltpu.make_async_copy(rows.at[k], out.at[:, (3 + k) * head : (4 + k) * head, :], done.at[k])
        copy.start()
        copies.append(copy)
    for copy in copies:
        copy.wait()


def stage_kernel(latents, out):
    pltpu.sync_copy(latents, out)


def pick_kernel(turn, frame, held, *rest):
    *arrived, out = rest
    which = which_of(frame[0], turn)
    for k, ref in enumerate((held, *arrived)):

        @pl.when(which == k)
        def _():
            out[...] = ref[...]


def first_kernel(frame, held, *rest):
    *arrived, gain, w_key, w_value, out, latents = rest
    pick_kernel(2, frame, held, *arrived, latents)
    head = latents.shape[1] // HEADS
    normed = normed_of(latents[...], gain[...])
    out[:, :head, :] = by_head(project(normed, w_key[...]))
    out[:, head:, :] = by_head(project(normed, w_value[...]))


def joined(ref, start, size, blocks):
    return jnp.concatenate([ref[b, start : start + size, :] for b in blocks], axis=1)


def ones_row(count):
    return (lax.broadcasted_iota(jnp.int32, (SPREAD, count), 0) == 0).astype(jnp.float32).astype(jnp.bfloat16)


def scores_of(key, query):
    return lax.dot_general(key, query, (((0,), (0,)), ((), ())), preferred_element_type=jnp.float32)


GROUP = 8


def near_kernel(rows, peak, total, queries):
    blocks, _, width = rows.shape
    head = rows.shape[1] // 5
    every = range(blocks)
    keys = [joined(rows, start * head, head, every) for start in (1, 3)]
    values = [
        jnp.concatenate([joined(rows, start * head, head, every), ones_row(blocks * width)], axis=0)
        for start in (2, 4)
    ]
    for g in range(0, blocks, GROUP):
        query = joined(rows, 0, head, range(g, g + GROUP))
        queries[:, g * width : (g + GROUP) * width] = query
        scores = [scores_of(key, query) for key in keys]
        top = jnp.maximum(*[jnp.max(s, axis=0, keepdims=True) for s in scores])
        span = slice(g * width, (g + GROUP) * width)
        peak[:, span] = jnp.broadcast_to(top, (8, GROUP * width))
        total[:, span] = sum(
            jnp.dot(value, jnp.exp2(s - top).astype(jnp.bfloat16), preferred_element_type=jnp.float32)
            for value, s in zip(values, scores)
        )


FAR = 60.0


def far_kernel(queries, first, peak, total, out, sums):
    blocks, _, width = first.shape
    head = queries.shape[0]
    every = range(blocks)
    key = joined(first, 0, head, every)
    value = jnp.concatenate([joined(first, head, head, every), ones_row(blocks * width)], axis=0)
    before = peak[:1, :]

    def weighted(scores, top):
        weights = jnp.exp2(scores - top).astype(jnp.bfloat16)
        return jnp.dot(value, weights, preferred_element_type=jnp.float32)

    scores = scores_of(key, queries[...])
    top = jnp.max(scores, axis=0, keepdims=True)
    sums[...] = total[...] + weighted(scores, before)

    @pl.when(jnp.max(top - before) > FAR)
    def _():
        both = jnp.maximum(top, before)
        sums[...] = total[...] * jnp.exp2(before - both) + weighted(scores_of(key, queries[...]), both)

    attended = (sums[:head, :] * (1.0 / sums[head : head + 1, :])).astype(jnp.bfloat16)
    for b in every:
        out[b] = attended[:, b * width : (b + 1) * width]


def mix_kernel(attended, latents, w_out, out):
    heads, head, positions = attended.shape
    rows = attended[...].reshape(heads * head, positions).T
    update = jnp.dot(rows, w_out[...], preferred_element_type=jnp.float32)
    out[...] = (latents[...].astype(jnp.float32) + update).astype(jnp.bfloat16)


def call(kernel, name, shapes, operands, kinds, to=pltpu.VMEM, scratch=(), flops=0, moved=0):
    spaces = {"s": pltpu.SMEM, "v": pltpu.VMEM, "a": pl.ANY}
    return pl.pallas_call(
        kernel,
        out_shape=shapes,
        in_specs=[pl.BlockSpec(memory_space=spaces[kind]) for kind in kinds],
        out_specs=jax.tree.map(lambda _: pl.BlockSpec(memory_space=to), shapes),
        scratch_shapes=list(scratch),
        compiler_params=pltpu.CompilerParams(vmem_limit_bytes=VMEM),
        cost_estimate=pl.CostEstimate(flops=int(flops), bytes_accessed=int(moved), transcendentals=0),
        name=name,
    )(*operands)


def body(latents, norm_gain, w_query, w_key, w_value, w_out):
    _, positions, channels = latents.shape
    head = channels // HEADS
    own = latents[0]
    frames = lax.axis_size("frame")
    at = lax.axis_index("frame")[None]
    total_positions = lax.axis_size("row") * positions

    def shape(*dims, kind=jnp.bfloat16):
        return jax.ShapeDtypeStruct(dims, kind)

    def send(array, turn):
        return [lax.ppermute(array, "frame", pairs_of(*permute)) for permute in ROUNDS[turn]]

    arrived = send(own, 0)
    prior = lax.ppermute(own, "frame", [(i, i + 1) for i in range(frames - 1)])
    own = call(stage_kernel, "stage", shape(positions, channels), (own,), "a", flops=COST_STAGE)
    held_a = call(
        functools.partial(pick_kernel, 0), "pick_a", shape(positions, channels),
        (at, own, *arrived), "svvvv", flops=COST_A,
    )
    arrived = send(held_a, 1)
    held_b = call(
        functools.partial(pick_kernel, 1), "pick_b", shape(positions, channels),
        (at, held_a, *arrived), "svvvvv", flops=COST_B,
    )
    arrived = send(held_b, 2)

    mine = call(
        own_kernel, "own_rows", shape(HEADS, 3 * head, positions),
        (own, norm_gain, w_query, w_key, w_value), "vvvvv",
        flops=2 * positions * channels * channels * 3, moved=3 * 2 * channels * channels,
    )
    mine = call(
        prior_kernel, "prior_rows", shape(HEADS, 5 * head, positions),
        (at, mine, own, prior, norm_gain, w_key, w_value, held_a), "svvvvvva", to=pl.ANY,
        scratch=[pltpu.VMEM((2, HEADS, head, positions), jnp.bfloat16), pltpu.SemaphoreType.DMA((3,))],
        flops=2 * positions * channels * channels * 2, moved=2 * 2 * channels * channels,
    )
    rows = lax.all_to_all(mine, "row", 0, 0, tiled=True)
    wide = (shape(8, total_positions, kind=jnp.float32), shape(head + SPREAD, total_positions, kind=jnp.float32))
    peak, total, queries = call(
        near_kernel, "near", (*wide, shape(head, total_positions)), (rows,), "v",
        flops=8 * head * total_positions * total_positions, moved=2 * 8 * 5 * head * positions,
    )
    theirs = call(
        first_kernel, "first_rows", shape(HEADS, 2 * head, positions),
        (at, held_b, *arrived, norm_gain, w_key, w_value), "svvvvvvv",
        scratch=[pltpu.VMEM((positions, channels), jnp.bfloat16)],
        flops=2 * positions * channels * channels * 2, moved=2 * 2 * channels * channels,
    )
    first = lax.all_to_all(theirs, "row", 0, 0, tiled=True)
    attended = call(
        far_kernel, "far", shape(HEADS, head, positions), (queries, first, peak, total), "vvvv",
        scratch=[pltpu.VMEM((head + SPREAD, total_positions), jnp.float32)],
        flops=4 * head * total_positions * total_positions, moved=2 * 8 * 2 * head * positions,
    )
    back = lax.all_to_all(attended, "row", 0, 0, tiled=True)
    mixed = call(
        mix_kernel, "mix", shape(positions, channels), (back, own, w_out), "vvv",
        flops=2 * positions * channels * channels, moved=2 * channels * channels,
    )
    return mixed[None]


def solution(mesh):
    return jax.shard_map(
        body,
        mesh=mesh,
        in_specs=(P("frame", "row", None), P(), P(), P(), P(), P()),
        out_specs=P("frame", "row", None),
        check_vma=False,
    )
```
